32 devices in a mesh: dp: 4 (over z), expert: 8 (over y, x, core).
Axes of the slice: x: 2, y: 2, z: 4, core: 2. Of those that a mesh axis runs over, the one named last changes fastest.
Arguments:
- inputs: bfloat16 [4096, 3584], P(('dp', 'expert')), may hold values from -6 to 6
- out_grad: bfloat16 [4096, 3584], P(('dp', 'expert')), may hold values from -6 to 6
- expert_ids: int32 [4096, 2], P(('dp', 'expert')), may hold values from 0 to 7, all different within a row; in each aligned block of 128 rows (0 to 127, 128 to 255, ...) at most 48 rows name the same one
- gates: bfloat16 [4096, 2], P(('dp', 'expert')), may hold values from 0.099609375 to 1
- w_gate: bfloat16 [8, 1024, 3584], P('expert'), may hold values from -0.09375 to 0.09375
- w_up: bfloat16 [8, 1024, 3584], P('expert'), may hold values from -0.09375 to 0.09375
- w_down: bfloat16 [8, 1024, 3584], P('expert'), may hold values from -0.1875 to 0.1875
Outputs:
- input_grad: bfloat16 [4096, 3584], P(('dp', 'expert'))
- gate_grad: bfloat16 [4096, 2], P(('dp', 'expert'))
- grad_gate: bfloat16 [8, 1024, 3584], P('expert', 'dp')
- grad_up: bfloat16 [8, 1024, 3584], P('expert', 'dp')
- grad_down: bfloat16 [8, 1024, 3584], P('expert', 'dp')
The draws below stay inside these ranges and needn't reach their ends.
Inputs may be any that keep to these rules, and one draw needn't show every extreme that they name: `expert_ids`: within the 128 rows of one device, no expert is named by more than 48 pairs, and in every draw some device names some expert exactly 48 times; a token's 2 experts differ.
All inputs are finite; a program needn't handle non-finite values.
Results may differ from the reference program's by a relative error of at most 0.013.
Values may be sent and summed in bfloat16 or wider, within the bound.
A program may use at most 192 MiB of HBM per device.

```python
import math
import jax
import jax.numpy as jnp
import numpy as np
from jax import lax

D = 3584
FF = 1024
TOP = 2
TOK_DEV = 128
CAP = 48
EXPERTS = 8
TOKENS = 4096
N_DP = 4
N_EXPERT = 8


def block_scale(stream_key, dims, cuts, low, top_value):
    def one(dim, parts):
        heights = jax.random.uniform(jax.random.fold_in(jax.random.fold_in(stream_key, 6), dim), (parts,), jnp.float32, low / len(cuts), top_value / len(cuts))
        return jnp.repeat(jnp.exp(heights), dims[dim] // parts).reshape((-1,) + (1,) * (len(dims) - dim - 1))

    loudness = one(*cuts[0])
    for cut in cuts[1:]:
        loudness = loudness * one(*cut)
    return loudness


def shared_out(own_key, own, number, rows, number_of, top, reach, skew):
    sequence = jax.random.permutation(own_key, number_of)
    crowded, usual = load_shares(number_of, rows * top, reach, skew, True), load_shares(number_of, rows * top, reach, skew, False)
    places = jnp.arange(number_of)

    def named(lengths, offset_by):
        used = int((lengths > 0).sum())
        fixed = max(1, used // 4)
        shifted = fixed + (places - fixed + offset_by * (used - fixed)) % max(1, number_of - fixed)
        return jnp.zeros((number_of,), jnp.int32).at[sequence[jnp.where(places < fixed, places, shifted)]].set(jnp.asarray(lengths, jnp.int32))

    lengths = jnp.where(number % 4 == 0, named(crowded, number // 4), named(usual, number - number // 4 - 1))
    mixed = jax.random.permutation(jax.random.fold_in(own, 3), number_of)
    giver, taker = mixed[0:number_of // 2 * 2:2], mixed[1:number_of // 2 * 2:2]
    slack = jnp.minimum(lengths[giver] - 1, reach - lengths[taker]) // 2
    slack = jnp.where((giver == sequence[0]) | (taker == sequence[0]) | (lengths[taker] == 0), 0, jnp.maximum(slack, 0))
    shifted = jax.random.randint(jax.random.fold_in(own, 4), (number_of // 2,), 0, 1 << 20) % (slack + 1)
    lengths = lengths.at[giver].add(-shifted).at[taker].add(shifted)
    labels = jnp.searchsorted(jnp.cumsum(lengths), jnp.arange(rows * top), side="right").astype(jnp.int32)
    table = labels.reshape(top, rows).T
    table = table[jax.random.permutation(jax.random.fold_in(own, 1), rows)]
    offset_by = jax.random.randint(jax.random.fold_in(own, 2), (rows, 1), 0, top)
    return jnp.take_along_axis(table, (jnp.arange(top)[None, :] + offset_by) % top, axis=1)


def load_shares(count, total, bound, lean, full):
    portions = [(1 << 20) // math.isqrt(standing ** lean) + 1 for standing in range(1, count + 1)]
    largest = bound if full else min(bound, max(-(-total // count), total * portions[0] // sum(portions)))
    least = 1 if total - largest >= count - 1 else 0
    holding, rest = [largest] + [least] * (count - 1), total - largest - least * (count - 1)
    while rest > 0:
        candidates = [i for i in range(1, count) if holding[i] < largest] or [i for i in range(1, count) if holding[i] < bound]
        pool, left = sum([portions[i] for i in candidates]), rest
        for i in candidates:
            addition = min(bound - holding[i], max(1, left * portions[i] // pool), rest)
            holding[i] = holding[i] + addition
            rest = rest - addition
    return np.array(holding)


def normal_values(key, extent, spread, reach, pieces=(), kind=jnp.bfloat16):
    values = spread * jax.random.normal(key, extent, jnp.float32)
    if pieces:
        values = values * block_scale(key, extent, pieces, -0.22, 0.18)
    return jnp.clip(values, -reach, reach).astype(kind)


def setup_inputs(seed: int = 0) -> dict:
    keys = jax.random.split(jax.random.key(seed), 8)
    inputs = normal_values(keys[0], (TOKENS, D), 1.0, 6.0, ((0, 32),))
    out_grad = normal_values(keys[1], (TOKENS, D), 1.0, 6.0, ((0, 32),))
    expert_ids_keys = jax.random.split(jax.random.fold_in(keys[2], 1), TOKENS // TOK_DEV)
    expert_ids_turns = jax.random.permutation(jax.random.fold_in(keys[2], 3), TOKENS // TOK_DEV)
    expert_ids = jax.vmap(lambda own, number: shared_out(jax.random.fold_in(keys[2], 2), own, number, TOK_DEV, EXPERTS, TOP, CAP, 2))(expert_ids_keys, expert_ids_turns).reshape((TOKENS, TOP))
    gates = jnp.clip(0.099609375 + 0.9003906 * jax.random.uniform(keys[3], (TOKENS, TOP), jnp.float32) ** block_scale(keys[3], (TOKENS, TOP), ((0, 32),), -0.2, 0.2), 0.099609375, 1.0).astype(jnp.bfloat16)
    w_gate = normal_values(keys[4], (EXPERTS, FF, D), D ** -0.5, 0.09375, ((0, 8),))
    w_up = normal_values(keys[5], (EXPERTS, FF, D), D ** -0.5, 0.09375, ((0, 8),))
    w_down = normal_values(keys[6], (EXPERTS, FF, D), FF ** -0.5, 0.1875, ((0, 8),))
    return {"inputs": inputs, "out_grad": out_grad, "expert_ids": expert_ids, "gates": gates, "w_gate": w_gate, "w_up": w_up, "w_down": w_down}


def build_tables(expert_ids, expert_count, capacity):
    token_count, top_count = expert_ids.shape
    flat_ids = expert_ids.reshape(-1)
    columns = jnp.arange(expert_count, dtype=jnp.int32)
    onehot = (flat_ids[:, None] == columns[None, :]).astype(jnp.int32)
    earlier = jnp.cumsum(onehot, axis=0) - onehot
    position = jnp.sum(earlier * onehot, axis=1).astype(jnp.int32)
    slot_index = flat_ids * capacity + position
    slot_range = jnp.arange(expert_count * capacity, dtype=jnp.int32)
    pair_table = (slot_index[:, None] == slot_range[None, :]).astype(jnp.bfloat16)
    token_table = jnp.sum(pair_table.reshape(token_count, top_count, -1).astype(jnp.float32), axis=1).astype(jnp.bfloat16)
    return pair_table, token_table


def contract_rows(left, right):
    return lax.dot_general(left, right, (((0,), (0,)), ((), ())), preferred_element_type=jnp.float32)


def times_weight(rows, weight):
    return lax.dot_general(rows, weight, (((1,), (1,)), ((), ())), preferred_element_type=jnp.float32)


def expert_pass(row_inputs, row_out_grads, row_gates, gate_matrix, up_matrix, down_matrix):
    gate_col = row_gates.astype(jnp.float32)[:, None]
    hidden_gate = times_weight(row_inputs, gate_matrix)
    hidden_up = times_weight(row_inputs, up_matrix)
    sigma = jax.nn.sigmoid(hidden_gate)
    activation = (hidden_gate * sigma * hidden_up).astype(jnp.bfloat16)
    scaled = (gate_col * row_out_grads.astype(jnp.float32)).astype(jnp.bfloat16)
    raw_grad = times_weight(row_out_grads, down_matrix)
    act_grad = gate_col * raw_grad
    gate_hidden = (act_grad * hidden_up * sigma * (1.0 + hidden_gate * (1.0 - sigma))).astype(jnp.bfloat16)
    up_hidden = (act_grad * hidden_gate * sigma).astype(jnp.bfloat16)
    row_back = (jnp.dot(gate_hidden, gate_matrix, preferred_element_type=jnp.float32)
                + jnp.dot(up_hidden, up_matrix, preferred_element_type=jnp.float32)).astype(jnp.bfloat16)
    expert_out = jnp.dot(activation, down_matrix, preferred_element_type=jnp.float32)
    pair_value = jnp.sum(row_out_grads.astype(jnp.float32) * expert_out, axis=1).astype(jnp.bfloat16)
    partials = jnp.stack([contract_rows(gate_hidden, row_inputs).astype(jnp.bfloat16),
                          contract_rows(up_hidden, row_inputs).astype(jnp.bfloat16),
                          contract_rows(activation, scaled).astype(jnp.bfloat16)])
    return row_back, pair_value, partials


def reference(inputs, out_grad, expert_ids, gates, w_gate, w_up, w_down):
    groups = N_DP
    owners = N_EXPERT
    devices_all = groups * owners
    ids_dev = expert_ids.reshape(devices_all, TOK_DEV, TOP)
    pair_tables, token_tables = jax.vmap(lambda block: build_tables(block, owners, CAP))(ids_dev)
    inputs_dev = inputs.reshape(devices_all, TOK_DEV, D)
    grads_dev = out_grad.reshape(devices_all, TOK_DEV, D)
    gates_dev = gates.reshape(devices_all, TOK_DEV * TOP)
    sent_inputs = jax.vmap(lambda table, rows: contract_rows(table, rows).astype(jnp.bfloat16))(token_tables, inputs_dev)
    sent_grads = jax.vmap(lambda table, rows: contract_rows(table, rows).astype(jnp.bfloat16))(token_tables, grads_dev)
    sent_gates = jax.vmap(lambda table, values: jnp.dot(values, table, preferred_element_type=jnp.float32).astype(jnp.bfloat16))(pair_tables, gates_dev)

    def to_owner(sent, tail):
        shaped = sent.reshape((groups, owners, owners, CAP) + tail)
        order = (2, 0, 1, 3) + tuple(range(4, 4 + len(tail)))
        return jnp.transpose(shaped, order).reshape((owners, groups, owners * CAP) + tail)

    owner_inputs = to_owner(sent_inputs, (D,))
    owner_grads = to_owner(sent_grads, (D,))
    owner_gates = to_owner(sent_gates, ())

    def one_expert(packed):
        x_groups, y_groups, g_groups, gate_matrix, up_matrix, down_matrix = packed

        def one_group(total, group):
            row_inputs, row_out_grads, row_gates = group
            row_back, pair_value, partials = expert_pass(row_inputs, row_out_grads, row_gates, gate_matrix, up_matrix, down_matrix)
            return total + partials.astype(jnp.float32), (row_back, pair_value)

        start = jnp.zeros((3, FF, D), jnp.float32)
        total, outputs = lax.scan(one_group, start, (x_groups, y_groups, g_groups))
        return total.astype(jnp.bfloat16), outputs[0], outputs[1]

    grads_all, backs, values = lax.map(one_expert, (owner_inputs, owner_grads, owner_gates, w_gate, w_up, w_down))
    backs = jnp.transpose(backs.reshape(owners, groups, owners, CAP, D), (1, 2, 0, 3, 4)).reshape(devices_all, owners * CAP, D)
    values = jnp.transpose(values.reshape(owners, groups, owners, CAP), (1, 2, 0, 3)).reshape(devices_all, owners * CAP)
    input_grad = jax.vmap(lambda table, rows: jnp.dot(table, rows, preferred_element_type=jnp.float32).astype(jnp.bfloat16))(token_tables, backs)
    gate_grad = jax.vmap(lambda table, vals: jnp.dot(table, vals, preferred_element_type=jnp.float32).astype(jnp.bfloat16))(pair_tables, values)
    return (input_grad.reshape(TOKENS, D), gate_grad.reshape(TOKENS, TOP),
            grads_all[:, 0], grads_all[:, 1], grads_all[:, 2])
```

```python
import jax
import jax.numpy as jnp
from jax import lax
from jax.sharding import PartitionSpec as P


def build_tables(expert_ids, expert_count, capacity):
    token_count, top_count = expert_ids.shape
    pair_count = token_count * top_count
    flat_ids = expert_ids.reshape(-1)
    columns = jnp.arange(expert_count, dtype=jnp.int32)
    onehot = flat_ids[:, None] == columns[None, :]
    rank = jnp.arange(pair_count, dtype=jnp.int32)
    before = (rank[:, None] > rank[None, :]).astype(jnp.bfloat16)
    earlier = jnp.dot(before, onehot.astype(jnp.bfloat16), preferred_element_type=jnp.float32)
    position = jnp.sum(jnp.where(onehot, earlier, 0.0), axis=1).astype(jnp.int32)
    slot_index = flat_ids * capacity + position
    slot_range = jnp.arange(expert_count * capacity, dtype=jnp.int32)
    pair_table = (slot_index[:, None] == slot_range[None, :]).astype(jnp.bfloat16)
    token_table = jnp.sum(
        pair_table.reshape(token_count, top_count, -1).astype(jnp.float32), axis=1
    ).astype(jnp.bfloat16)
    return (pair_table, token_table)


def contract_rows(left, right):
    return lax.dot_general(
        left, right, (((0,), (0,)), ((), ())), preferred_element_type=jnp.float32
    )


def times_weight(rows, weight):
    return lax.dot_general(
        rows, weight, (((1,), (1,)), ((), ())), preferred_element_type=jnp.float32
    )


def exchange(rows, axis):
    return lax.all_to_all(rows, axis, split_axis=0, concat_axis=0, tiled=True)


def shards(inputs, out_grad, expert_ids, gates, w_gate, w_up, w_down):
    token_count, width = inputs.shape
    top_count = expert_ids.shape[1]
    expert_count = lax.axis_size("expert")
    group_count = lax.axis_size("dp")
    own_group = lax.axis_index("dp")
    capacity = 3 * token_count * top_count // (2 * expert_count)
    hidden = w_gate.shape[1]
    part = hidden // group_count

    all_ids = lax.all_gather(expert_ids, "dp", tiled=False)
    all_inputs = lax.all_gather(inputs, "dp", tiled=False)

    pair_table, token_table = build_tables(expert_ids, expert_count, capacity)

    def to_slots(table, rows):
        return (
            contract_rows(table, rows)
            .astype(jnp.bfloat16)
            .reshape(expert_count, capacity, width)
        )

    sent_gates = (
        jnp.dot(gates.reshape(-1), pair_table, preferred_element_type=jnp.float32)
        .astype(jnp.bfloat16)
        .reshape(expert_count, capacity)
    )
    row_inputs = exchange(to_slots(token_table, inputs), "expert").reshape(-1, width)
    row_out_grads = exchange(to_slots(token_table, out_grad), "expert").reshape(-1, width)
    gate_col = exchange(sent_gates, "expert").reshape(-1).astype(jnp.float32)[:, None]

    gate_matrix = w_gate[0]
    up_matrix = w_up[0]
    down_matrix = w_down[0]
    hidden_gate = times_weight(row_inputs, gate_matrix)
    hidden_up = times_weight(row_inputs, up_matrix)
    sigma = jax.nn.sigmoid(hidden_gate)
    activation = hidden_gate * sigma * hidden_up
    scaled_activation = (gate_col * activation).astype(jnp.bfloat16)
    down_sum = lax.psum_scatter(
        contract_rows(scaled_activation, row_out_grads).astype(jnp.bfloat16),
        "dp",
        scatter_dimension=0,
        tiled=True,
    )

    raw_grad = times_weight(row_out_grads, down_matrix)
    act_grad = gate_col * raw_grad
    gate_hidden = (act_grad * hidden_up * sigma * (1.0 + hidden_gate * (1.0 - sigma))).astype(
        jnp.bfloat16
    )
    up_hidden = (act_grad * hidden_gate * sigma).astype(jnp.bfloat16)
    pair_value = jnp.sum(
        activation.astype(jnp.bfloat16).astype(jnp.float32) * raw_grad, axis=1
    )
    pair_value = pair_value.astype(jnp.bfloat16).reshape(expert_count, capacity)

    row_back = (
        jnp.dot(gate_hidden, gate_matrix, preferred_element_type=jnp.float32)
        + jnp.dot(up_hidden, up_matrix, preferred_element_type=jnp.float32)
    ).astype(jnp.bfloat16)
    back_rows = exchange(row_back.reshape(expert_count, capacity, width), "expert")
    back_values = exchange(pair_value, "expert")

    joint_hidden = jnp.concatenate(
        [
            gate_hidden.reshape(-1, group_count, part),
            up_hidden.reshape(-1, group_count, part),
        ],
        axis=2,
    )
    joint_hidden = exchange(jnp.transpose(joint_hidden, (1, 0, 2)), "dp")

    other_rows = []
    for step in range(1, group_count):
        group = lax.rem(own_group + step, group_count)
        ids = lax.dynamic_index_in_dim(all_ids, group, 0, keepdims=False)
        tokens = lax.dynamic_index_in_dim(all_inputs, group, 0, keepdims=False)
        table = build_tables(ids, expert_count, capacity)[1]
        other_rows.append(exchange(to_slots(table, tokens), "expert").reshape(-1, width))

    joint = contract_rows(
        lax.dynamic_index_in_dim(joint_hidden, own_group, 0, keepdims=False), row_inputs
    )
    for step in range(1, group_count):
        group = lax.rem(own_group + step, group_count)
        joint = joint + contract_rows(
            lax.dynamic_index_in_dim(joint_hidden, group, 0, keepdims=False),
            other_rows[step - 1],
        )
    joint = joint.astype(jnp.bfloat16)

    input_grad = jnp.dot(
        token_table, back_rows.reshape(-1, width), preferred_element_type=jnp.float32
    ).astype(jnp.bfloat16)
    gate_grad = (
        jnp.dot(pair_table, back_values.reshape(-1), preferred_element_type=jnp.float32)
        .astype(jnp.bfloat16)
        .reshape(token_count, top_count)
    )
    return (
        input_grad,
        gate_grad,
        joint[:part][None],
        joint[part:][None],
        down_sum[None],
    )


def solution(mesh):
    in_specs = (
        P(("dp", "expert"), None),
        P(("dp", "expert"), None),
        P(("dp", "expert"), None),
        P(("dp", "expert"), None),
        P("expert", None, None),
        P("expert", None, None),
        P("expert", None, None),
    )
    out_specs = (
        P(("dp", "expert"), None),
        P(("dp", "expert"), None),
        P("expert", "dp", None),
        P("expert", "dp", None),
        P("expert", "dp", None),
    )
    return jax.shard_map(shards, mesh=mesh, in_specs=in_specs, out_specs=out_specs, check_vma=False)
```

```python
import jax
import jax.numpy as jnp
from jax import lax
from jax.sharding import PartitionSpec as P


def build_tables(expert_ids, expert_count, capacity):
    token_count, top_count = expert_ids.shape
    pair_count = token_count * top_count
    flat_ids = expert_ids.reshape(-1)
    columns = jnp.arange(expert_count, dtype=jnp.int32)
    onehot = flat_ids[:, None] == columns[None, :]
    rank = jnp.arange(pair_count, dtype=jnp.int32)
    before = (rank[:, None] > rank[None, :]).astype(jnp.bfloat16)
    earlier = jnp.dot(before, onehot.astype(jnp.bfloat16), preferred_element_type=jnp.float32)
    position = jnp.sum(jnp.where(onehot, earlier, 0.0), axis=1).astype(jnp.int32)
    slot_index = flat_ids * capacity + position
    slot_range = jnp.arange(expert_count * capacity, dtype=jnp.int32)
    pair_table = (slot_index[:, None] == slot_range[None, :]).astype(jnp.bfloat16)
    token_table = jnp.sum(
        pair_table.reshape(token_count, top_count, -1).astype(jnp.float32), axis=1
    ).astype(jnp.bfloat16)
    return (pair_table, token_table)


def contract_rows(left, right):
    return lax.dot_general(
        left, right, (((0,), (0,)), ((), ())), preferred_element_type=jnp.float32
    )


def times_weight(rows, weight):
    return lax.dot_general(
        rows, weight, (((1,), (1,)), ((), ())), preferred_element_type=jnp.float32
    )


def exchange(rows, axis):
    return lax.all_to_all(rows, axis, split_axis=0, concat_axis=0, tiled=True)


def shards(inputs, out_grad, expert_ids, gates, w_gate, w_up, w_down):
    token_count, width = inputs.shape
    top_count = expert_ids.shape[1]
    expert_count = lax.axis_size("expert")
    group_count = lax.axis_size("dp")
    own_group = lax.axis_index("dp")
    capacity = 3 * token_count * top_count // (2 * expert_count)
    hidden = w_gate.shape[1]
    part = hidden // group_count

    def from_group(values, step):
        pairs = [((i + step) % group_count, i) for i in range(group_count)]
        return lax.ppermute(values, "dp", pairs)

    other_ids = [from_group(expert_ids, step) for step in range(1, group_count)]
    all_inputs = lax.all_gather(inputs, "dp", tiled=False)

    pair_table, token_table = build_tables(expert_ids, expert_count, capacity)
    gated_table = jnp.sum(
        (pair_table * gates.reshape(-1)[:, None])
        .reshape(token_count, top_count, -1)
        .astype(jnp.float32),
        axis=1,
    ).astype(jnp.bfloat16)

    def to_slots(table, rows):
        return (
            contract_rows(table, rows)
            .astype(jnp.bfloat16)
            .reshape(expert_count, capacity, width)
        )

    row_inputs = exchange(to_slots(token_table, inputs), "expert").reshape(-1, width)
    scaled = exchange(to_slots(gated_table, out_grad), "expert").reshape(-1, width)

    gate_matrix = w_gate[0]
    up_matrix = w_up[0]
    down_matrix = w_down[0]
    hidden_gate = times_weight(row_inputs, gate_matrix)
    hidden_up = times_weight(row_inputs, up_matrix)
    sigma = jax.nn.sigmoid(hidden_gate)
    activation = lax.optimization_barrier(
        (hidden_gate * sigma * hidden_up).astype(jnp.bfloat16)
    )
    down_partial = contract_rows(activation, scaled).astype(jnp.bfloat16)
    down_sum = lax.psum_scatter(down_partial, "dp", scatter_dimension=0, tiled=True)
    late_scaled = lax.optimization_barrier((scaled, down_partial))[0]

    other_rows = []
    after = scaled
    for step in range(1, group_count):
        group = lax.rem(own_group + step, group_count)
        tokens = lax.dynamic_index_in_dim(all_inputs, group, 0, keepdims=False)
        table = build_tables(other_ids[step - 1], expert_count, capacity)[1]
        sent = lax.optimization_barrier((to_slots(table, tokens), after))[0]
        after = exchange(sent, "expert").reshape(-1, width)
        other_rows.append(after)

    act_grad = times_weight(late_scaled, down_matrix)
    gate_hidden = (act_grad * hidden_up * sigma * (1.0 + hidden_gate * (1.0 - sigma))).astype(
        jnp.bfloat16
    )
    up_hidden = (act_grad * hidden_gate * sigma).astype(jnp.bfloat16)
    gated_value = jnp.sum(activation.astype(jnp.float32) * act_grad, axis=1)
    gated_value = gated_value.astype(jnp.bfloat16).reshape(expert_count, capacity)

    def hidden_part(group):
        return jnp.concatenate(
            [
                lax.dynamic_slice_in_dim(values, group * part, part, axis=1)
                for values in (gate_hidden, up_hidden)
            ],
            axis=1,
        )

    other_hidden = [
        from_group(hidden_part(lax.rem(own_group + group_count - step, group_count)), step)
        for step in range(1, group_count)
    ]

    row_back = (
        jnp.dot(gate_hidden, gate_matrix, preferred_element_type=jnp.float32)
        + jnp.dot(up_hidden, up_matrix, preferred_element_type=jnp.float32)
    ).astype(jnp.bfloat16)
    row_back, gated_value = lax.optimization_barrier((row_back, gated_value, after))[:2]
    back_rows = exchange(row_back.reshape(expert_count, capacity, width), "expert")
    back_values = exchange(gated_value, "expert")

    joint = contract_rows(hidden_part(own_group), row_inputs)
    for rows, values in zip(other_rows, other_hidden):
        joint = joint + contract_rows(values, rows)
    joint = joint.astype(jnp.bfloat16)

    input_grad = jnp.dot(
        token_table, back_rows.reshape(-1, width), preferred_element_type=jnp.float32
    ).astype(jnp.bfloat16)
    gate_grad = (
        jnp.dot(pair_table, back_values.reshape(-1), preferred_element_type=jnp.float32)
        .reshape(token_count, top_count)
        / gates.astype(jnp.float32)
    ).astype(jnp.bfloat16)
    return (
        input_grad,
        gate_grad,
        joint[:part][None],
        joint[part:][None],
        down_sum[None],
    )


def solution(mesh):
    in_specs = (
        P(("dp", "expert"), None),
        P(("dp", "expert"), None),
        P(("dp", "expert"), None),
        P(("dp", "expert"), None),
        P("expert", None, None),
        P("expert", None, None),
        P("expert", None, None),
    )
    out_specs = (
        P(("dp", "expert"), None),
        P(("dp", "expert"), None),
        P("expert", "dp", None),
        P("expert", "dp", None),
        P("expert", "dp", None),
    )
    return jax.shard_map(shards, mesh=mesh, in_specs=in_specs, out_specs=out_specs, check_vma=False)
```

```python
import jax
import jax.numpy as jnp
from jax import lax
from jax.sharding import PartitionSpec as P


def build_tables(expert_ids, expert_count, capacity):
    token_count, top_count = expert_ids.shape
    pair_count = token_count * top_count
    flat_ids = expert_ids.reshape(-1)
    columns = jnp.arange(expert_count, dtype=jnp.int32)
    onehot = flat_ids[:, None] == columns[None, :]
    rank = jnp.arange(pair_count, dtype=jnp.int32)
    before = (rank[:, None] > rank[None, :]).astype(jnp.bfloat16)
    earlier = jnp.dot(before, onehot.astype(jnp.bfloat16), preferred_element_type=jnp.float32)
    position = jnp.sum(jnp.where(onehot, earlier, 0.0), axis=1).astype(jnp.int32)
    slot_index = flat_ids * capacity + position
    slot_range = jnp.arange(expert_count * capacity, dtype=jnp.int32)
    pair_table = (slot_index[:, None] == slot_range[None, :]).astype(jnp.bfloat16)
    token_table = jnp.sum(
        pair_table.reshape(token_count, top_count, -1).astype(jnp.float32), axis=1
    ).astype(jnp.bfloat16)
    return (pair_table, token_table)


def contract_rows(left, right):
    return lax.dot_general(
        left, right, (((0,), (0,)), ((), ())), preferred_element_type=jnp.float32
    )


def times_weight(rows, weight):
    return lax.dot_general(
        rows, weight, (((1,), (1,)), ((), ())), preferred_element_type=jnp.float32
    )


def exchange(rows, axis):
    return lax.all_to_all(rows, axis, split_axis=0, concat_axis=0, tiled=True)


def shards(inputs, out_grad, expert_ids, gates, w_gate, w_up, w_down):
    token_count, width = inputs.shape
    top_count = expert_ids.shape[1]
    expert_count = lax.axis_size("expert")
    group_count = lax.axis_size("dp")
    own_group = lax.axis_index("dp")
    capacity = 3 * token_count * top_count // (2 * expert_count)
    hidden = w_gate.shape[1]
    part = hidden // group_count

    def from_group(values, step):
        pairs = [((i + step) % group_count, i) for i in range(group_count)]
        return lax.ppermute(values, "dp", pairs)

    other_ids = [from_group(expert_ids, step) for step in range(1, group_count)]
    all_inputs = lax.all_gather(inputs, "dp", tiled=False)

    pair_table, token_table = build_tables(expert_ids, expert_count, capacity)
    gated_table = jnp.sum(
        (pair_table * gates.reshape(-1)[:, None])
        .reshape(token_count, top_count, -1)
        .astype(jnp.float32),
        axis=1,
    ).astype(jnp.bfloat16)

    def to_slots(table, rows):
        return (
            contract_rows(table, rows)
            .astype(jnp.bfloat16)
            .reshape(expert_count, capacity, width)
        )

    other_tables = [build_tables(ids, expert_count, capacity)[1] for ids in other_ids]

    def other_slots(step):
        tokens = lax.dynamic_index_in_dim(
            all_inputs, lax.rem(own_group + step, group_count), 0, keepdims=False
        )
        return to_slots(other_tables[step - 1], tokens)

    row_inputs = exchange(to_slots(token_table, inputs), "expert").reshape(-1, width)
    sent_scaled, other_tables = lax.optimization_barrier(
        (to_slots(gated_table, out_grad), other_tables)
    )
    scaled = exchange(sent_scaled, "expert").reshape(-1, width)

    gate_matrix = w_gate[0]
    up_matrix = w_up[0]
    down_matrix = w_down[0]
    hidden_gate = times_weight(row_inputs, gate_matrix)
    hidden_up = times_weight(row_inputs, up_matrix)
    sigma = jax.nn.sigmoid(hidden_gate)
    activation = lax.optimization_barrier(
        (hidden_gate * sigma * hidden_up).astype(jnp.bfloat16)
    )
    scaled, sent = lax.optimization_barrier((scaled, other_slots(1)))
    down_partial = contract_rows(activation, scaled).astype(jnp.bfloat16)
    down_sum = lax.psum_scatter(down_partial, "dp", scatter_dimension=0, tiled=True)
    late_scaled = lax.optimization_barrier((scaled, down_partial))[0]

    act_grad = times_weight(late_scaled, down_matrix)
    gate_hidden = (act_grad * hidden_up * sigma * (1.0 + hidden_gate * (1.0 - sigma))).astype(
        jnp.bfloat16
    )
    up_hidden = (act_grad * hidden_gate * sigma).astype(jnp.bfloat16)
    gated_value = jnp.sum(activation.astype(jnp.float32) * act_grad, axis=1)
    gated_value = gated_value.astype(jnp.bfloat16).reshape(expert_count, capacity)

    def hidden_part(group):
        return jnp.concatenate(
            [
                lax.dynamic_slice_in_dim(values, group * part, part, axis=1)
                for values in (gate_hidden, up_hidden)
            ],
            axis=1,
        )

    parts = [
        hidden_part(lax.rem(own_group + group_count - step, group_count))
        for step in range(1, group_count)
    ]
    parts = lax.optimization_barrier(parts)
    other_hidden = [from_group(values, step + 1) for step, values in enumerate(parts)]

    row_back = (
        jnp.dot(gate_hidden, gate_matrix, preferred_element_type=jnp.float32)
        + jnp.dot(up_hidden, up_matrix, preferred_element_type=jnp.float32)
    ).astype(jnp.bfloat16)

    other_rows = [exchange(sent, "expert")]
    ready = parts
    for step in range(2, group_count):
        if step == group_count - 1:
            row_back, gated_value, ready = lax.optimization_barrier(
                (row_back, gated_value, (other_rows[-1], other_hidden[0]))
            )
            back_rows = exchange(row_back.reshape(expert_count, capacity, width), "expert")
            back_values = exchange(gated_value, "expert")
            ready = (back_rows, back_values, other_hidden)
        sent = lax.optimization_barrier((other_slots(step), other_rows[-1], ready))[0]
        other_rows.append(exchange(sent, "expert"))
        ready = ()
    other_hidden = lax.optimization_barrier((other_hidden, sent))[0]

    joint = contract_rows(hidden_part(own_group), row_inputs)
    for rows, values in zip(other_rows, other_hidden):
        joint = joint + contract_rows(values, rows.reshape(-1, width))
    joint = joint.astype(jnp.bfloat16)

    input_grad = jnp.dot(
        token_table, back_rows.reshape(-1, width), preferred_element_type=jnp.float32
    ).astype(jnp.bfloat16)
    gate_grad = (
        jnp.dot(pair_table, back_values.reshape(-1), preferred_element_type=jnp.float32)
        .reshape(token_count, top_count)
        / gates.astype(jnp.float32)
    ).astype(jnp.bfloat16)
    return (
        input_grad,
        gate_grad,
        joint[:part][None],
        joint[part:][None],
        down_sum[None],
    )


def solution(mesh):
    in_specs = (
        P(("dp", "expert"), None),
        P(("dp", "expert"), None),
        P(("dp", "expert"), None),
        P(("dp", "expert"), None),
        P("expert", None, None),
        P("expert", None, None),
        P("expert", None, None),
    )
    out_specs = (
        P(("dp", "expert"), None),
        P(("dp", "expert"), None),
        P("expert", "dp", None),
        P("expert", "dp", None),
        P("expert", "dp", None),
    )
    return jax.shard_map(shards, mesh=mesh, in_specs=in_specs, out_specs=out_specs, check_vma=False)
```

```python
import jax
import jax.numpy as jnp
from jax import lax
from jax.sharding import PartitionSpec as P


def build_tables(expert_ids, expert_count, capacity):
    token_count, top_count = expert_ids.shape
    pair_count = token_count * top_count
    flat_ids = expert_ids.reshape(-1)
    columns = jnp.arange(expert_count, dtype=jnp.int32)
    onehot = flat_ids[:, None] == columns[None, :]
    rank = jnp.arange(pair_count, dtype=jnp.int32)
    before = (rank[:, None] > rank[None, :]).astype(jnp.bfloat16)
    earlier = jnp.dot(before, onehot.astype(jnp.bfloat16), preferred_element_type=jnp.float32)
    position = jnp.sum(jnp.where(onehot, earlier, 0.0), axis=1).astype(jnp.int32)
    slot_index = flat_ids * capacity + position
    slot_range = jnp.arange(expert_count * capacity, dtype=jnp.int32)
    pair_table = (slot_index[:, None] == slot_range[None, :]).astype(jnp.bfloat16)
    token_table = jnp.sum(
        pair_table.reshape(token_count, top_count, -1).astype(jnp.float32), axis=1
    ).astype(jnp.bfloat16)
    return (pair_table, token_table)


def contract_rows(left, right):
    return lax.dot_general(
        left, right, (((0,), (0,)), ((), ())), preferred_element_type=jnp.float32
    )


def times_weight(rows, weight):
    return lax.dot_general(
        rows, weight, (((1,), (1,)), ((), ())), preferred_element_type=jnp.float32
    )


def exchange(rows, axis):
    return lax.all_to_all(rows, axis, split_axis=0, concat_axis=0, tiled=True)


def shards(inputs, out_grad, expert_ids, gates, w_gate, w_up, w_down):
    token_count, width = inputs.shape
    top_count = expert_ids.shape[1]
    expert_count = lax.axis_size("expert")
    group_count = lax.axis_size("dp")
    own_group = lax.axis_index("dp")
    capacity = 3 * token_count * top_count // (2 * expert_count)
    hidden = w_gate.shape[1]
    part = hidden // group_count

    def from_group(values, step):
        pairs = [((i + step) % group_count, i) for i in range(group_count)]
        return lax.ppermute(values, "dp", pairs)

    other_ids = [from_group(expert_ids, step) for step in range(1, group_count)]
    all_inputs = lax.all_gather(inputs, "dp", tiled=False)

    pair_table, token_table = build_tables(expert_ids, expert_count, capacity)
    gated_table = jnp.sum(
        (pair_table * gates.reshape(-1)[:, None])
        .reshape(token_count, top_count, -1)
        .astype(jnp.float32),
        axis=1,
    ).astype(jnp.bfloat16)

    def to_slots(table, rows):
        return (
            contract_rows(table, rows)
            .astype(jnp.bfloat16)
            .reshape(expert_count, capacity, width)
        )

    other_tables = [build_tables(ids, expert_count, capacity)[1] for ids in other_ids]

    def other_slots(step):
        tokens = lax.dynamic_index_in_dim(
            all_inputs, lax.rem(own_group + step, group_count), 0, keepdims=False
        )
        return to_slots(other_tables[step - 1], tokens)

    row_inputs = exchange(to_slots(token_table, inputs), "expert").reshape(-1, width)
    sent_scaled, other_tables = lax.optimization_barrier(
        (to_slots(gated_table, out_grad), other_tables)
    )
    scaled = exchange(sent_scaled, "expert").reshape(-1, width)

    gate_matrix = w_gate[0]
    up_matrix = w_up[0]
    down_matrix = w_down[0]
    hidden_gate = times_weight(row_inputs, gate_matrix)
    hidden_up = times_weight(row_inputs, up_matrix)
    sigma = jax.nn.sigmoid(hidden_gate)
    activation = lax.optimization_barrier(
        (hidden_gate * sigma * hidden_up).astype(jnp.bfloat16)
    )
    scaled, sent = lax.optimization_barrier((scaled, other_slots(1)))
    down_partial = contract_rows(activation, scaled).astype(jnp.bfloat16)
    down_sum = lax.psum_scatter(down_partial, "dp", scatter_dimension=0, tiled=True)
    late_scaled = lax.optimization_barrier((scaled, down_partial))[0]

    act_grad = times_weight(late_scaled, down_matrix)
    gate_hidden = (act_grad * hidden_up * sigma * (1.0 + hidden_gate * (1.0 - sigma))).astype(
        jnp.bfloat16
    )
    up_hidden = (act_grad * hidden_gate * sigma).astype(jnp.bfloat16)
    gated_value = jnp.sum(activation.astype(jnp.float32) * act_grad, axis=1)
    gated_value = gated_value.astype(jnp.bfloat16).reshape(expert_count, capacity)

    def hidden_part(group):
        return jnp.concatenate(
            [
                lax.dynamic_slice_in_dim(values, group * part, part, axis=1)
                for values in (gate_hidden, up_hidden)
            ],
            axis=1,
        )

    parts = [
        hidden_part(lax.rem(own_group + group_count - step, group_count))
        for step in range(1, group_count)
    ]
    parts = lax.optimization_barrier(parts)
    other_hidden = [from_group(values, step + 1) for step, values in enumerate(parts)]

    row_back = (
        jnp.dot(gate_hidden, gate_matrix, preferred_element_type=jnp.float32)
        + jnp.dot(up_hidden, up_matrix, preferred_element_type=jnp.float32)
    ).astype(jnp.bfloat16)

    other_rows = [exchange(sent, "expert")]
    ready = parts
    for step in range(2, group_count):
        if step == group_count - 1:
            row_back, gated_value, ready = lax.optimization_barrier(
                (row_back, gated_value, (other_rows[-1], other_hidden[:2]))
            )
            back_rows = exchange(row_back.reshape(expert_count, capacity, width), "expert")
            back_values = exchange(gated_value, "expert")
            ready = (back_rows, back_values, other_hidden)
        sent = lax.optimization_barrier((other_slots(step), other_rows[-1], ready))[0]
        other_rows.append(exchange(sent, "expert"))
        ready = ()
    other_hidden = lax.optimization_barrier((other_hidden, sent))[0]

    joint = contract_rows(hidden_part(own_group), row_inputs)
    for rows, values in zip(other_rows, other_hidden):
        joint = joint + contract_rows(values, rows.reshape(-1, width))
    joint = joint.astype(jnp.bfloat16)

    input_grad = jnp.dot(
        token_table, back_rows.reshape(-1, width), preferred_element_type=jnp.float32
    ).astype(jnp.bfloat16)
    gate_grad = (
        jnp.dot(pair_table, back_values.reshape(-1), preferred_element_type=jnp.float32)
        .reshape(token_count, top_count)
        / gates.astype(jnp.float32)
    ).astype(jnp.bfloat16)
    return (
        input_grad,
        gate_grad,
        joint[:part][None],
        joint[part:][None],
        down_sum[None],
    )


def solution(mesh):
    in_specs = (
        P(("dp", "expert"), None),
        P(("dp", "expert"), None),
        P(("dp", "expert"), None),
        P(("dp", "expert"), None),
        P("expert", None, None),
        P("expert", None, None),
        P("expert", None, None),
    )
    out_specs = (
        P(("dp", "expert"), None),
        P(("dp", "expert"), None),
        P("expert", "dp", None),
        P("expert", "dp", None),
        P("expert", "dp", None),
    )
    return jax.shard_map(shards, mesh=mesh, in_specs=in_specs, out_specs=out_specs, check_vma=False)
```
